32 devices in a mesh: group: 2 (over y), hid: 4 (over z), wid: 4 (over x, core).
Axes of the slice: x: 2, y: 2, z: 4, core: 2. Of those that a mesh axis runs over, the one named last changes fastest.
Arguments:
- tokens: bfloat16 [256, 8192], P(('group', 'hid'), 'wid'), parts along dimension 0, may hold values from -6 to 6
- gate_weight: bfloat16 [8192, 26624], P('wid', 'hid'), may hold values from -0.0625 to 0.0625
- up_weight: bfloat16 [8192, 26624], P('wid', 'hid'), may hold values from -0.0625 to 0.0625
- down_weight: bfloat16 [26624, 8192], P('hid', 'wid'), may hold values from -0.0390625 to 0.0390625
Outputs:
- mixed: bfloat16 [256, 8192], P(('group', 'hid'), 'wid'), parts along dimension 0
The draws below stay inside these ranges and needn't reach their ends.
There are 2 independent parts, one for each index of `group`. The reference program is written for one: setup_inputs(seed, part) draws one part's arguments, and reference() takes and returns one part's arrays. A program takes and returns all parts, laid end to end along the dimension named above; an argument that names none is the same for every part. Nothing has to cross between parts.
All inputs are finite; a program needn't handle non-finite values.
Results may differ from the reference program's by a relative error of at most 0.005.
Values may be sent and summed in bfloat16 or wider, within the bound.
No kernel may reach another device: no remote copies, remote signals or barrier semaphores. Data moves between devices by JAX's collectives and lax.ppermute only.
A program may use at most 192 MiB of HBM per device.

```python
import jax
import jax.numpy as jnp

D = 8192
FF = 26624
TOKENS = 128


def block_levels(own_key, extent, cuts, smallest, largest):
    def one(dim, blocks):
        steps = jax.random.uniform(jax.random.fold_in(jax.random.fold_in(own_key, 6), dim), (blocks,), jnp.float32, smallest / len(cuts), largest / len(cuts))
        return jnp.repeat(jnp.exp(steps), extent[dim] // blocks).reshape((-1,) + (1,) * (len(extent) - dim - 1))

    level = one(*cuts[0])
    for cut in cuts[1:]:
        level = level * one(*cut)
    return level


def bell_draw(key, extent, scale, limit, cuts=(), kind=jnp.bfloat16):
    result = jax.random.normal(key, extent, jnp.float32) * scale
    if len(cuts) > 0:
        result = block_levels(key, extent, cuts, -0.22, 0.18) * result
    return jnp.clip(result, min=-limit, max=limit).astype(kind)


def setup_inputs(seed: int = 0, part: int = 0) -> dict:
    key_list = jax.random.split(jax.random.key(seed), 5)
    part_keys = jax.random.split(jax.random.fold_in(key_list[4], part), 5)
    return {
        "tokens": bell_draw(part_keys[0], (TOKENS, D), 1.0, 6.0, ((0, 4), (1, 4))),
        "gate_weight": bell_draw(key_list[1], (D, FF), D ** -0.5, 0.0625, ((0, 4), (1, 4))),
        "up_weight": bell_draw(key_list[2], (D, FF), D ** -0.5, 0.0625, ((0, 4), (1, 4))),
        "down_weight": bell_draw(key_list[3], (FF, D), FF ** -0.5, 0.0390625, ((0, 4), (1, 4))),
    }


def reference(tokens, gate_weight, up_weight, down_weight):
    gate = jnp.dot(tokens, gate_weight, preferred_element_type=jnp.float32)
    up = jnp.dot(tokens, up_weight, preferred_element_type=jnp.float32)
    hidden = (jax.nn.silu(gate) * up).astype(jnp.bfloat16)
    return jnp.dot(hidden, down_weight, preferred_element_type=jnp.float32).astype(jnp.bfloat16)
```

```python
import functools

import jax
import jax.numpy as jnp
from jax import lax
from jax.experimental import pallas as pl
from jax.experimental.pallas import tpu as pltpu
from jax.sharding import PartitionSpec as P

MIB = 1 << 20
WHOLE = pl.BlockSpec(memory_space=pltpu.VMEM)
STAY = pl.BlockSpec(memory_space=pl.ANY)


def largest(total, options):
    return next(o for o in options if total % o == 0)


def call(kernel, ins, outs, scratch, flops, moved, limit):
    return pl.pallas_call(
        kernel,
        in_specs=ins,
        out_specs=[WHOLE] * len(outs),
        out_shape=outs,
        scratch_shapes=scratch,
        compiler_params=pltpu.CompilerParams(vmem_limit_bytes=limit),
        cost_estimate=pl.CostEstimate(flops=flops, bytes_accessed=moved, transcendentals=0),
    )


def gate_up_kernel(start, width, depth, slots, blocks, *refs):
    parts, (gate_ref, up_ref, send_ref, keep_ref, left, held, sems) = refs[:blocks], refs[blocks:]
    steps = left.shape[1] // depth
    total = 2 * steps

    def copy(i):
        source = (gate_ref, up_ref)[i % 2]
        slot = i % slots
        return pltpu.make_async_copy(
            source.at[pl.ds(i // 2 * depth, depth), pl.ds(start, width)], held.at[slot], sems.at[slot]
        )

    for i in range(min(slots, total)):
        copy(i).start()
    rows = parts[0].shape[0]
    half = left.shape[0] // 2
    other = 1 - lax.rem(lax.axis_index("wid"), 2)
    for j, part in enumerate(parts):
        at = lax.rem(j * rows + other * half, 2 * half)
        left[pl.ds(pl.multiple_of(at, rows), rows), :] = part[...]
    sums = [None, None]
    for i in range(total):
        copy(i).wait()
        product = jnp.dot(
            left[:, pl.ds(i // 2 * depth, depth)], held[i % slots], preferred_element_type=jnp.float32
        )
        sums[i % 2] = product if i < 2 else sums[i % 2] + product
        if i + slots < total:
            copy(i + slots).start()
    for which in range(2):
        send_ref[which] = sums[which][:half].astype(jnp.bfloat16)
        keep_ref[which] = sums[which][half:]


def chip_sum_kernel(count, keep_ref, came_ref, own_ref, *send_refs):
    rows = own_ref.shape[1]
    me = lax.axis_index("wid") // 2
    for j in range(count):
        at = pl.ds(pl.multiple_of(lax.rem(me + j, count) * rows, rows), rows)
        for which in range(2):
            value = keep_ref[which, at, :] + came_ref[which, at, :].astype(jnp.float32)
            if j == 0:
                own_ref[which] = value
            else:
                send_refs[j - 1][which] = value.astype(jnp.bfloat16)


def hidden_kernel(own_ref, *refs):
    came_refs, hidden_ref = refs[:-1], refs[-1]
    gate, up = own_ref[0], own_ref[1]
    for came in came_refs:
        gate = gate + came[0].astype(jnp.float32)
        up = up + came[1].astype(jnp.float32)
    hidden_ref[...] = (gate / (1.0 + jnp.exp(-gate)) * up).astype(jnp.bfloat16)


def down_kernel(start, depth, slots, count, first, last, *refs):
    pieces, refs = refs[: 2 * count], refs[2 * count :]
    if not first:
        before_ref, refs = refs[0], refs[1:]
    down_ref, refs = refs[0], refs[1:]
    outs, (left, held, sems) = refs[:-3], refs[-3:]
    total = left.shape[1] // depth

    def copy(i):
        slot = i % slots
        return pltpu.make_async_copy(down_ref.at[pl.ds(start + i * depth, depth), :], held.at[slot], sems.at[slot])

    for i in range(min(slots, total)):
        copy(i).start()
    rows = pieces[0].shape[0]
    half = left.shape[0] // 2
    x, core = lax.axis_index("wid") // 2, lax.rem(lax.axis_index("wid"), 2)
    for side in range(2):
        for j in range(count):
            base = (core if side == 0 else 1 - core) * half
            at = base + lax.rem(x - j + count, count) * rows
            left[pl.ds(pl.multiple_of(at, rows), rows), :] = pieces[side * count + j][...]
    value = None if first else before_ref[...]
    for i in range(total):
        copy(i).wait()
        product = jnp.dot(left[:, pl.ds(i * depth, depth)], held[i % slots], preferred_element_type=jnp.float32)
        value = product if value is None else value + product
        if i + slots < total:
            copy(i + slots).start()
    if not last:
        outs[0][...] = value
    else:
        rows = outs[0].shape[0]
        for j, out in enumerate(outs):
            out[...] = value[j * rows : (j + 1) * rows].astype(out.dtype)


def final_kernel(own_ref, *refs):
    value = own_ref[...]
    for came in refs[:-1]:
        value = value + came[...].astype(jnp.float32)
    refs[-1][...] = value.astype(refs[-1].dtype)


def body(groups, wide, tokens, gate_weight, up_weight, down_weight):
    chips = wide // 2
    f32, bf16 = jnp.float32, jnp.bfloat16
    shape = jax.ShapeDtypeStruct
    part, width = tokens.shape
    units = gate_weight.shape[1]
    rows = part * groups
    own_rows = rows // wide

    other_core = [(w, w ^ 1) for w in range(wide)]

    def along_x(value, j):
        return lax.ppermute(value, "wid", [(w, (w // 2 + j) % chips * 2 + w % 2) for w in range(wide)])

    def along_z(value, j):
        return lax.ppermute(value, "hid", [(z, (z + j) % groups) for z in range(groups)])

    step = units // 26 if units // 26 % 128 == 0 else units // 13
    count = units // step
    cuts = [0, count * 6 // 26, count * 16 // 26, count]
    chunks = [(a * step, (b - a) * step) for a, b in zip(cuts[:-1], cuts[1:])]

    parts = [tokens] + [along_z(tokens, groups - j) for j in range(1, groups)]

    summed = []
    for start, size in chunks:
        depth = largest(width, (512, 256))
        slots = 6
        send, keep = call(
            functools.partial(gate_up_kernel, start, size, depth, slots, groups),
            [WHOLE] * groups + [STAY] * 2,
            [shape((2, rows // 2, size), bf16), shape((2, rows // 2, size), f32)],
            [pltpu.VMEM((rows, width), bf16), pltpu.VMEM((slots, depth, size), bf16), pltpu.SemaphoreType.DMA((slots,))],
            4 * rows * width * size,
            4 * width * size,
            34 * MIB,
        )(*parts, gate_weight, up_weight)
        came = lax.ppermute(send, "wid", other_core)
        summed.append((keep, came))

    hidden = []
    for (keep, came), (start, size) in zip(summed, chunks):
        own, *sends = call(
            functools.partial(chip_sum_kernel, chips),
            [WHOLE] * 2,
            [shape((2, own_rows, size), f32)] + [shape((2, own_rows, size), bf16)] * (chips - 1),
            [],
            rows * size,
            4 * rows * size,
            24 * MIB,
        )(keep, came)
        arrived = [along_x(sends[j - 1], j) for j in range(1, chips)]
        (mine,) = call(
            hidden_kernel, [WHOLE] * chips, [shape((own_rows, size), bf16)], [], own_rows * size * 8, 8 * own_rows * size, 24 * MIB
        )(own, *arrived)
        near = [mine] + [along_x(mine, j) for j in range(1, chips)]
        far = [lax.ppermute(v, "wid", other_core) for v in near]
        hidden.append(near + far)

    value = []
    for n, (pieces, (start, size)) in enumerate(zip(hidden, chunks)):
        first, last = n == 0, n == len(chunks) - 1
        depth = largest(size, (512, 256, 128))
        slots = 5
        outs = [shape((part, width), f32)] + [shape((part, width), bf16)] * (groups - 1) if last else [shape((rows, width), f32)]
        value = call(
            functools.partial(down_kernel, start, depth, slots, chips, first, last),
            [WHOLE] * (len(pieces) + len(value)) + [STAY],
            outs,
            [pltpu.VMEM((rows, size), bf16), pltpu.VMEM((slots, depth, width), bf16), pltpu.SemaphoreType.DMA((slots,))],
            2 * rows * width * size,
            2 * width * size,
            28 * MIB,
        )(*pieces, *value, down_weight)

    arrived = [along_z(value[j], j) for j in range(1, groups)]
    (mixed,) = call(final_kernel, [WHOLE] * groups, [shape((part, width), bf16)], [], groups * part * width, 4 * groups * part * width, 16 * MIB)(
        value[0], *arrived
    )
    return mixed


def solution(mesh):
    placed = (P(("group", "hid"), "wid"), P("wid", "hid"), P("wid", "hid"), P("hid", "wid"))
    return jax.shard_map(
        functools.partial(body, mesh.shape["hid"], mesh.shape["wid"]),
        mesh=mesh,
        in_specs=placed,
        out_specs=P(("group", "hid"), "wid"),
        check_vma=False,
    )
```

```python
import functools

import jax
import jax.numpy as jnp
from jax import lax
from jax.experimental import pallas as pl
from jax.experimental.pallas import tpu as pltpu
from jax.sharding import PartitionSpec as P

MIB = 1 << 20
F32, BF16 = jnp.float32, jnp.bfloat16
WHOLE = pl.BlockSpec(memory_space=pltpu.VMEM)
FAR = pl.BlockSpec(memory_space=pltpu.HBM)
STAY = pl.BlockSpec(memory_space=pl.ANY)
NEAR_ROWS, FAR_ROWS = 0, 1


def largest(total, options):
    return next(o for o in options if total % o == 0)


def fetch_start(copies):
    for copy in copies:
        copy.start()


def fetch_wait(copies):
    for copy in copies:
        copy.wait()


def column_copies(start, sources, targets, sems):
    pieces = sems.shape[0] // 2
    depth = targets[0].shape[0] // pieces
    copies = []
    for i in range(2 * pieces):
        at = pl.ds(i // 2 * depth, depth)
        source, target = sources[i % 2], targets[i % 2]
        copies.append(
            pltpu.make_async_copy(source.at[at, pl.ds(start, target.shape[1])], target.at[at, :], sems.at[i])
        )
    return copies


def fetch_kernel(start, gate_ref, up_ref, gate_out, up_out, sems):
    copies = column_copies(start, (gate_ref, up_ref), (gate_out, up_out), sems)
    fetch_start(copies)
    fetch_wait(copies)


def order_rows(parts, left):
    rows = parts[0][0].shape[0]
    half = len(parts[0]) * rows
    other = 1 - lax.rem(lax.axis_index("wid"), 2)
    for h, blocks in enumerate(parts):
        for j, block in enumerate(blocks):
            at = h * half + lax.rem(j * rows + other * (half // 2), half)
            left[pl.ds(pl.multiple_of(at, rows), rows), :] = block[...]


def put_sums(sums, halves, send_refs, keep_ref):
    for which, value in enumerate(sums):
        quarter = value.shape[0] // (2 * halves)
        for h in range(halves):
            at = 2 * h * quarter
            send_refs[h % len(send_refs)][h // len(send_refs), which] = value[at : at + quarter].astype(BF16)
            keep_ref[h, which] = value[at + quarter : at + 2 * quarter]


def split_parts(refs, halves, blocks):
    return [refs[h * blocks : (h + 1) * blocks] for h in range(halves)], refs[halves * blocks :]


def held_gate_up_kernel(halves, blocks, *refs):
    parts, (gate_ref, up_ref, *send_refs, keep_ref, left) = split_parts(refs, halves, blocks)
    order_rows(parts, left)
    sums = [jnp.dot(left[...], w[...], preferred_element_type=F32) for w in (gate_ref, up_ref)]
    put_sums(sums, halves, send_refs, keep_ref)


def gate_up_kernel(start, width, depth, slots, halves, blocks, *refs):
    parts, (gate_ref, up_ref, *send_refs, keep_ref, left, held, sems) = split_parts(refs, halves, blocks)
    total = 2 * (left.shape[1] // depth)

    def copy(i):
        source = (gate_ref, up_ref)[i % 2]
        slot = i % slots
        return pltpu.make_async_copy(
            source.at[pl.ds(i // 2 * depth, depth), pl.ds(start, width)], held.at[slot], sems.at[slot]
        )

    for i in range(min(slots, total)):
        copy(i).start()
    order_rows(parts, left)
    sums = [None, None]
    for i in range(total):
        copy(i).wait()
        product = jnp.dot(left[:, pl.ds(i // 2 * depth, depth)], held[i % slots], preferred_element_type=F32)
        sums[i % 2] = product if i < 2 else sums[i % 2] + product
        if i + slots < total:
            copy(i + slots).start()
    put_sums(sums, halves, send_refs, keep_ref)


def chip_sum_kernel(chips, halves, keep, *refs):
    came, outs = refs[:-chips], refs[-chips:]
    rows = outs[0].shape[2]
    me = lax.axis_index("wid") // 2
    for j in range(chips):
        at = pl.ds(pl.multiple_of(lax.rem(me + j, chips) * rows, rows), rows)
        for h in range(halves):
            for which in range(2):
                other = came[h % len(came)][h // len(came), which, at, :]
                outs[j][h, which] = (keep[h, which, at, :] + other.astype(F32)).astype(outs[j].dtype)


def hidden_kernel(own_ref, *refs):
    came_refs, hidden_ref = refs[:-1], refs[-1]
    for h in range(own_ref.shape[0]):
        gate, up = own_ref[h, 0], own_ref[h, 1]
        for came in came_refs:
            gate = gate + came[h, 0].astype(F32)
            up = up + came[h, 1].astype(F32)
        hidden_ref[h] = (gate / (1.0 + jnp.exp(-gate)) * up).astype(BF16)


def pack_kernel(*refs):
    for j, ref in enumerate(refs[:-1]):
        refs[-1][j] = ref[...]


def fetch_rows_kernel(start, down_ref, out_ref, sems):
    pieces = sems.shape[0]
    rows = out_ref.shape[0] // pieces
    copies = [
        pltpu.make_async_copy(
            down_ref.at[pl.ds(start + p * rows, rows), :], out_ref.at[pl.ds(p * rows, rows), :], sems.at[p]
        )
        for p in range(pieces)
    ]
    fetch_start(copies)
    fetch_wait(copies)


def place_hidden(pairs, left):
    x, core = lax.axis_index("wid") // 2, lax.rem(lax.axis_index("wid"), 2)
    for side, ref in enumerate(pairs):
        chips, halves, rows, _ = ref.shape
        quarter = left.shape[0] // (2 * halves)
        for h in range(halves):
            for j in range(chips):
                base = (2 * h + (core if side == 0 else 1 - core)) * quarter
                at = base + lax.rem(x - j + chips, chips) * rows
                left[pl.ds(pl.multiple_of(at, rows), rows), :] = ref[j, h]


def down_kernel(first, last, near_ref, far_ref, *refs):
    if not first:
        before_ref, refs = refs[0], refs[1:]
    down_ref, outs, left = refs[0], refs[1:-1], refs[-1]
    place_hidden((near_ref, far_ref), left)
    value = jnp.dot(left[...], down_ref[...], preferred_element_type=F32)
    if not first:
        value = value + before_ref[...]
    rows = outs[0].shape[0]
    for j, out in enumerate(outs):
        out[...] = value[j * rows : (j + 1) * rows].astype(out.dtype)


def final_kernel(own_ref, *refs):
    value = own_ref[...]
    for came in refs[:-1]:
        value = value + came[...].astype(F32)
    refs[-1][...] = value.astype(refs[-1].dtype)


class Body:
    def __init__(self, groups, wide):
        self.groups, self.wide, self.chips = groups, wide, wide // 2
        self.last = None

    def call(self, kernel, ins, outs, scratch, flops, moved, limit, args):
        after = [] if self.last is None else [self.last]

        def run(*refs):
            kernel(*refs[len(after) :])

        got = pl.pallas_call(
            run,
            name=kernel.func.__name__ if isinstance(kernel, functools.partial) else kernel.__name__,
            in_specs=[STAY] * len(after) + ins,
            out_specs=[WHOLE] * len(outs),
            out_shape=outs,
            scratch_shapes=scratch,
            compiler_params=pltpu.CompilerParams(vmem_limit_bytes=limit),
            cost_estimate=pl.CostEstimate(flops=flops, bytes_accessed=moved, transcendentals=0),
        )(*after, *args)
        self.last = got[0]
        return got

    def other_core(self, value):
        return lax.ppermute(value, "wid", [(w, w ^ 1) for w in range(self.wide)])

    def along_x(self, value, j):
        return lax.ppermute(value, "wid", [(w, (w // 2 + j) % self.chips * 2 + w % 2) for w in range(self.wide)])

    def along_z(self, value, j):
        return lax.ppermute(value, "hid", [(z, z ^ j) for z in range(self.groups)])

    def gate_up(self, start, size, halves, weights, sends=1):
        width = self.width
        parts = [p for h in halves for p in self.parts[h]]
        rows = len(parts) * self.part
        quarter = rows // (2 * len(halves))
        outs = [jax.ShapeDtypeStruct((len(halves) // sends, 2, quarter, size), BF16)] * sends
        outs.append(jax.ShapeDtypeStruct((len(halves), 2, quarter, size), F32))
        left = pltpu.VMEM((rows, width), BF16)
        count = (len(halves), self.groups // 2)
        if weights is not None:
            got = self.call(
                functools.partial(held_gate_up_kernel, *count),
                [WHOLE] * (len(parts) + 2),
                outs,
                [left],
                4 * rows * width * size,
                rows * width,
                6 * MIB,
                (*parts, *weights),
            )
        else:
            depth, slots = largest(width, (512, 256)), 4
            got = self.call(
                functools.partial(gate_up_kernel, start, size, depth, slots, *count),
                [WHOLE] * len(parts) + [FAR] * 2,
                outs,
                [left, pltpu.VMEM((slots, depth, size), BF16), pltpu.SemaphoreType.DMA((slots,))],
                4 * rows * width * size,
                4 * width * size,
                16 * MIB,
                (*parts, self.gate_weight, self.up_weight),
            )
        return got[-1], *(self.other_core(v) for v in got[:-1])

    def fetch(self, start, size):
        return self.call(
            functools.partial(fetch_kernel, start),
            [FAR] * 2,
            [jax.ShapeDtypeStruct((self.width, size), BF16)] * 2,
            [pltpu.SemaphoreType.DMA((8,))],
            0,
            4 * self.width * size,
            2 * MIB,
            (self.gate_weight, self.up_weight),
        )

    def chip_sum(self, halves, args):
        size = args[0].shape[3]
        block = (len(halves), 2, self.block, size)
        own, *sends = self.call(
            functools.partial(chip_sum_kernel, self.chips, len(halves)),
            [WHOLE] * len(args),
            [jax.ShapeDtypeStruct(block, F32)] + [jax.ShapeDtypeStruct(block, BF16)] * (self.chips - 1),
            [],
            size * 256,
            size * 1024,
            4 * MIB,
            args,
        )
        return own, [self.along_x(v, j + 1) for j, v in enumerate(sends)]

    def hidden(self, summed):
        own, came = summed
        n, _, rows, size = own.shape
        (mine,) = self.call(
            hidden_kernel,
            [WHOLE] * (1 + len(came)),
            [jax.ShapeDtypeStruct((n, rows, size), BF16)],
            [],
            size * 256,
            size * 1024,
            4 * MIB,
            (own, *came),
        )
        return [mine] + [self.along_x(mine, j) for j in range(1, self.chips)]

    def pack(self, near):
        shape = jax.ShapeDtypeStruct((len(near),) + near[0].shape, BF16)
        (packed,) = self.call(pack_kernel, [WHOLE] * len(near), [shape], [], 256, 1024, 4 * MIB, near)
        return packed, self.other_core(packed)

    def fetch_rows(self, start, size):
        (rows,) = self.call(
            functools.partial(fetch_rows_kernel, start),
            [FAR],
            [jax.ShapeDtypeStruct((size, self.width), BF16)],
            [pltpu.SemaphoreType.DMA((4,))],
            0,
            2 * self.width * size,
            2 * MIB,
            (self.down_weight,),
        )
        return rows

    def down(self, packed, before, weights, last):
        size = weights.shape[0]
        width, rows = self.width, 2 * self.half
        if last:
            outs = [jax.ShapeDtypeStruct((self.part, width), t) for t in [F32] + [BF16] * (self.groups - 1)]
        else:
            outs = [jax.ShapeDtypeStruct((rows, width), F32)]
        return self.call(
            functools.partial(down_kernel, not before, last),
            [WHOLE] * (3 + len(before)),
            outs,
            [pltpu.VMEM((rows, size), BF16)],
            2 * rows * width * size,
            rows * size,
            6 * MIB,
            (*packed, *before, weights),
        )

    def __call__(self, tokens, gate_weight, up_weight, down_weight):
        self.gate_weight, self.up_weight, self.down_weight = (
            pltpu.with_memory_space_constraint(w, pltpu.HBM) for w in (gate_weight, up_weight, down_weight)
        )
        self.part, self.width = tokens.shape
        groups = self.groups
        self.half = self.part * groups // 2
        self.block = self.half // self.wide
        units = gate_weight.shape[1]
        step = units // 26 if units // 26 % 128 == 0 else units // 13
        count = units // step
        cuts = [count * c // 26 * step for c in (0, 9, 17, 26)]
        (s0, n0), (s1, n1), (s2, n2) = [(a, b - a) for a, b in zip(cuts[:-1], cuts[1:])]
        both = (NEAR_ROWS, FAR_ROWS)

        blocks = [tokens] + [self.along_z(tokens, j) for j in range(1, groups)]
        self.parts = (blocks[: groups // 2], blocks[groups // 2 :])

        w0 = self.fetch(s0, n0)
        w1 = self.fetch(s1, n1)
        a0 = self.gate_up(s0, n0, both, w0)
        a1 = self.gate_up(s1, n1, both, w1)
        b0 = self.chip_sum(both, a0)
        b1 = self.chip_sum(both, a1)
        a2 = self.gate_up(s2, n2, both, None, 2)
        h0 = self.hidden(b0)
        b2 = self.chip_sum(both, a2)
        d0 = self.fetch_rows(s0, n0)
        h1 = self.hidden(b1)
        d1 = self.fetch_rows(s1, n1)
        p0 = self.pack(h0)
        d2 = self.fetch_rows(s2, n2)
        h2 = self.hidden(b2)
        p1 = self.pack(h1)
        value = self.down(p0, [], d0, False)
        p2 = self.pack(h2)
        value = self.down(p1, value, d1, False)
        own, *late = self.down(p2, value, d2, True)
        arrived = [self.along_z(late[j - 1], j) for j in range(groups - 1, 0, -1)]
        (mixed,) = self.call(
            final_kernel,
            [WHOLE] * groups,
            [jax.ShapeDtypeStruct((self.part, self.width), BF16)],
            [],
            groups * self.part * self.width,
            4 * groups * self.part * self.width,
            4 * MIB,
            (own, *arrived),
        )
        return mixed


def solution(mesh):
    placed = (P(("group", "hid"), "wid"), P("wid", "hid"), P("wid", "hid"), P("hid", "wid"))

    def run(*arrays):
        return Body(mesh.shape["hid"], mesh.shape["wid"])(*arrays)

    return jax.shard_map(run, mesh=mesh, in_specs=placed, out_specs=P(("group", "hid"), "wid"), check_vma=False)
```

```python
import functools

import jax
import jax.numpy as jnp
from jax import lax
from jax.experimental import pallas as pl
from jax.experimental.pallas import tpu as pltpu
from jax.sharding import PartitionSpec as P

MIB = 1 << 20
F32, BF16 = jnp.float32, jnp.bfloat16
WHOLE = pl.BlockSpec(memory_space=pltpu.VMEM)
FAR = pl.BlockSpec(memory_space=pltpu.HBM)
STAY = pl.BlockSpec(memory_space=pl.ANY)
NEAR_ROWS, FAR_ROWS = 0, 1


def largest(total, options):
    return next(o for o in options if total % o == 0)


def fetch_start(copies):
    for copy in copies:
        copy.start()


def fetch_wait(copies):
    for copy in copies:
        copy.wait()


def column_copies(start, sources, targets, sems):
    pieces = sems.shape[0] // 2
    depth = targets[0].shape[0] // pieces
    copies = []
    for i in range(2 * pieces):
        at = pl.ds(i // 2 * depth, depth)
        source, target = sources[i % 2], targets[i % 2]
        copies.append(
            pltpu.make_async_copy(source.at[at, pl.ds(start, target.shape[1])], target.at[at, :], sems.at[i])
        )
    return copies


def fetch_kernel(start, gate_ref, up_ref, gate_out, up_out, sems):
    copies = column_copies(start, (gate_ref, up_ref), (gate_out, up_out), sems)
    fetch_start(copies)
    fetch_wait(copies)


def order_rows(parts, left):
    rows = parts[0][0].shape[0]
    half = len(parts[0]) * rows
    other = 1 - lax.rem(lax.axis_index("wid"), 2)
    for h, blocks in enumerate(parts):
        for j, block in enumerate(blocks):
            at = h * half + lax.rem(j * rows + other * (half // 2), half)
            left[pl.ds(pl.multiple_of(at, rows), rows), :] = block[...]


def put_sums(sums, halves, send_refs, keep_ref, column):
    for which, value in enumerate(sums):
        quarter = value.shape[0] // (2 * halves)
        columns = slice(column, column + value.shape[1])
        for h in range(halves):
            at = 2 * h * quarter
            send = send_refs[h % len(send_refs)]
            send[h // len(send_refs), which, :, columns] = value[at : at + quarter].astype(BF16)
            keep_ref[h, which, :, columns] = value[at + quarter : at + 2 * quarter]


def split_parts(refs, halves, blocks):
    return [refs[h * blocks : (h + 1) * blocks] for h in range(halves)], refs[halves * blocks :]


def held_gate_up_kernel(halves, blocks, ahead, *refs):
    parts, (gate_ref, up_ref, *refs) = split_parts(refs, halves, blocks)
    copies = []
    if ahead is not None:
        sources, refs, sems = refs[:2], refs[2:-1], refs[-1]
        copies = column_copies(ahead, sources, refs[2:4], sems)
        refs = refs[:2] + refs[4:]
    send_ref, keep_ref, left = refs
    fetch_start(copies)
    order_rows(parts, left)
    sums = [jnp.dot(left[...], w[...], preferred_element_type=F32) for w in (gate_ref, up_ref)]
    put_sums(sums, halves, [send_ref], keep_ref, 0)
    fetch_wait(copies)


def gate_up_kernel(start, width, depth, slots, halves, blocks, sends, *refs):
    parts, refs = split_parts(refs, halves, blocks)
    held_refs, (gate_ref, up_ref), refs = refs[:2], refs[2:4], refs[4:]
    send_refs, keep_ref, left, held, sems = refs[:sends], *refs[sends:]
    before = held_refs[0].shape[1]
    total = 2 * (left.shape[1] // depth)

    def copy(i):
        source = (gate_ref, up_ref)[i % 2]
        slot = i % slots
        return pltpu.make_async_copy(
            source.at[pl.ds(i // 2 * depth, depth), pl.ds(start + before, width - before)], held.at[slot], sems.at[slot]
        )

    for i in range(min(slots, total)):
        copy(i).start()
    order_rows(parts, left)
    sums = [jnp.dot(left[...], w[...], preferred_element_type=F32) for w in held_refs]
    put_sums(sums, halves, send_refs, keep_ref, 0)
    sums = [None, None]
    for i in range(total):
        copy(i).wait()
        product = jnp.dot(left[:, pl.ds(i // 2 * depth, depth)], held[i % slots], preferred_element_type=F32)
        sums[i % 2] = product if i < 2 else sums[i % 2] + product
        if i + slots < total:
            copy(i + slots).start()
    put_sums(sums, halves, send_refs, keep_ref, before)


def chip_sum_kernel(chips, halves, keep, *refs):
    came, outs = refs[:-chips], refs[-chips:]
    rows = outs[0].shape[2]
    me = lax.axis_index("wid") // 2
    for j in range(chips):
        at = pl.ds(pl.multiple_of(lax.rem(me + j, chips) * rows, rows), rows)
        for h in range(halves):
            for which in range(2):
                other = came[h % len(came)][h // len(came), which, at, :]
                outs[j][h, which] = (keep[h, which, at, :] + other.astype(F32)).astype(outs[j].dtype)


def hidden_kernel(own_ref, *refs):
    came_refs, hidden_ref = refs[:-1], refs[-1]
    for h in range(own_ref.shape[0]):
        gate, up = own_ref[h, 0], own_ref[h, 1]
        for came in came_refs:
            gate = gate + came[h, 0].astype(F32)
            up = up + came[h, 1].astype(F32)
        hidden_ref[h] = (gate / (1.0 + jnp.exp(-gate)) * up).astype(BF16)


def pack_kernel(*refs):
    for j, ref in enumerate(refs[:-1]):
        refs[-1][j] = ref[...]


def fetch_rows_kernel(start, down_ref, out_ref, sems):
    pieces = sems.shape[0]
    rows = out_ref.shape[0] // pieces
    copies = [
        pltpu.make_async_copy(
            down_ref.at[pl.ds(start + p * rows, rows), :], out_ref.at[pl.ds(p * rows, rows), :], sems.at[p]
        )
        for p in range(pieces)
    ]
    fetch_start(copies)
    fetch_wait(copies)


def place_hidden(pairs, left):
    x, core = lax.axis_index("wid") // 2, lax.rem(lax.axis_index("wid"), 2)
    for side, ref in enumerate(pairs):
        chips, halves, rows, _ = ref.shape
        quarter = left.shape[0] // (2 * halves)
        for h in range(halves):
            for j in range(chips):
                base = (2 * h + (core if side == 0 else 1 - core)) * quarter
                at = base + lax.rem(x - j + chips, chips) * rows
                left[pl.ds(pl.multiple_of(at, rows), rows), :] = ref[j, h]


def down_kernel(first, direct, near_ref, far_ref, *refs):
    if not first:
        before_ref, refs = refs[0], refs[1:]
    down_ref, outs, left = refs[0], refs[1:-1], refs[-1]
    place_hidden((near_ref, far_ref), left)
    value = jnp.dot(left[...], down_ref[...], preferred_element_type=F32)
    if not first:
        value = value + before_ref[...]
    if direct is None:
        outs[0][...] = value
        return
    own_ref, soon_ref, *late_refs = outs
    rows, width = own_ref.shape
    blocks = value.shape[0] // rows
    straight, held = late_refs[: blocks - 2], late_refs[blocks - 2 :]
    own_ref[...] = value[:rows]
    soon_ref[:, :width] = value[rows : 2 * rows].astype(BF16)
    for j in range(2, blocks):
        block = value[j * rows : (j + 1) * rows]
        straight[j - 2][...] = block[:, :direct].astype(BF16)
        if j % 2 == 0:
            held[j // 2 - 1][...] = block[:, direct:]
        else:
            at = width + (j // 2 - 1) * (width - direct)
            soon_ref[:, at : at + width - direct] = block[:, direct:].astype(BF16)


def pair_sum_kernel(width, soon_ref, *refs):
    count = len(refs) // 2
    for held, out in zip(refs[:count], refs[count:]):
        size = held.shape[1]
        out[...] = (held[...] + soon_ref[:, width : width + size].astype(F32)).astype(BF16)
        width += size


def final_kernel(direct, count, own_ref, soon_ref, *refs):
    straight, joined, out_ref = refs[:count], refs[count:-1], refs[-1]
    width = own_ref.shape[1]
    value = own_ref[...] + soon_ref[:, :width].astype(F32)
    for side, arrays in ((slice(0, direct), straight), (slice(direct, width), joined)):
        part = value[:, side]
        for came in arrays:
            part = part + came[...].astype(F32)
        out_ref[:, side] = part.astype(out_ref.dtype)


class Body:
    def __init__(self, groups, wide):
        self.groups, self.wide, self.chips = groups, wide, wide // 2
        self.last = None

    def call(self, kernel, ins, outs, scratch, flops, moved, limit, args):
        after = [] if self.last is None else [self.last]

        def run(*refs):
            kernel(*refs[len(after) :])

        got = pl.pallas_call(
            run,
            name=kernel.func.__name__ if isinstance(kernel, functools.partial) else kernel.__name__,
            in_specs=[STAY] * len(after) + ins,
            out_specs=[WHOLE] * len(outs),
            out_shape=outs,
            scratch_shapes=scratch,
            compiler_params=pltpu.CompilerParams(vmem_limit_bytes=limit),
            cost_estimate=pl.CostEstimate(flops=flops, bytes_accessed=moved, transcendentals=0),
        )(*after, *args)
        self.last = got[0]
        return got

    def other_core(self, value):
        return lax.ppermute(value, "wid", [(w, w ^ 1) for w in range(self.wide)])

    def along_x(self, value, j):
        return lax.ppermute(value, "wid", [(w, (w // 2 + j) % self.chips * 2 + w % 2) for w in range(self.wide)])

    def along_z(self, value, j):
        return lax.ppermute(value, "hid", [(z, z ^ j) for z in range(self.groups)])

    def gate_up_parts(self):
        parts = [p for h in self.parts for p in h]
        return parts, len(parts) * self.part

    def held_gate_up(self, weights, ahead):
        parts, rows = self.gate_up_parts()
        size = weights[0].shape[1]
        outs = [jax.ShapeDtypeStruct((2, 2, rows // 4, size), t) for t in (BF16, F32)]
        ins, more = [WHOLE] * (len(parts) + 2), ()
        scratch = [pltpu.VMEM((rows, self.width), BF16)]
        if ahead is not None:
            outs += [jax.ShapeDtypeStruct((self.width, ahead[1]), BF16)] * 2
            ins, more = ins + [FAR] * 2, (self.gate_weight, self.up_weight)
            scratch.append(pltpu.SemaphoreType.DMA((8,)))
        got = self.call(
            functools.partial(held_gate_up_kernel, 2, self.groups // 2, None if ahead is None else ahead[0]),
            ins,
            outs,
            scratch,
            4 * rows * self.width * size,
            rows * self.width,
            6 * MIB,
            (*parts, *weights, *more),
        )
        return (got[1], self.other_core(got[0])), got[2:]

    def gate_up(self, start, size, weights, sends):
        parts, rows = self.gate_up_parts()
        width = self.width
        outs = [jax.ShapeDtypeStruct((2 // sends, 2, rows // 4, size), BF16)] * sends
        outs.append(jax.ShapeDtypeStruct((2, 2, rows // 4, size), F32))
        depth, slots = largest(width, (512, 256)), 8
        streamed = size - weights[0].shape[1]
        got = self.call(
            functools.partial(gate_up_kernel, start, size, depth, slots, 2, self.groups // 2, sends),
            [WHOLE] * (len(parts) + 2) + [FAR] * 2,
            outs,
            [
                pltpu.VMEM((rows, width), BF16),
                pltpu.VMEM((slots, depth, streamed), BF16),
                pltpu.SemaphoreType.DMA((slots,)),
            ],
            4 * rows * width * size,
            4 * width * size,
            20 * MIB,
            (*parts, *weights, self.gate_weight, self.up_weight),
        )
        return got[-1], *(self.other_core(v) for v in got[:-1])

    def fetch(self, start, size):
        return self.call(
            functools.partial(fetch_kernel, start),
            [FAR] * 2,
            [jax.ShapeDtypeStruct((self.width, size), BF16)] * 2,
            [pltpu.SemaphoreType.DMA((8,))],
            0,
            4 * self.width * size,
            2 * MIB,
            (self.gate_weight, self.up_weight),
        )

    def chip_sum(self, halves, args):
        size = args[0].shape[3]
        block = (len(halves), 2, self.block, size)
        own, *sends = self.call(
            functools.partial(chip_sum_kernel, self.chips, len(halves)),
            [WHOLE] * len(args),
            [jax.ShapeDtypeStruct(block, F32)] + [jax.ShapeDtypeStruct(block, BF16)] * (self.chips - 1),
            [],
            size * 256,
            size * 1024,
            4 * MIB,
            args,
        )
        return own, [self.along_x(v, j + 1) for j, v in enumerate(sends)]

    def hidden(self, summed):
        own, came = summed
        n, _, rows, size = own.shape
        (mine,) = self.call(
            hidden_kernel,
            [WHOLE] * (1 + len(came)),
            [jax.ShapeDtypeStruct((n, rows, size), BF16)],
            [],
            size * 256,
            size * 1024,
            4 * MIB,
            (own, *came),
        )
        return [mine] + [self.along_x(mine, j) for j in range(1, self.chips)]

    def pack(self, near):
        shape = jax.ShapeDtypeStruct((len(near),) + near[0].shape, BF16)
        (packed,) = self.call(pack_kernel, [WHOLE] * len(near), [shape], [], 256, 1024, 4 * MIB, near)
        return packed, self.other_core(packed)

    def fetch_rows(self, start, size):
        (rows,) = self.call(
            functools.partial(fetch_rows_kernel, start),
            [FAR],
            [jax.ShapeDtypeStruct((size, self.width), BF16)],
            [pltpu.SemaphoreType.DMA((4,))],
            0,
            2 * self.width * size,
            2 * MIB,
            (self.down_weight,),
        )
        return rows

    def down(self, packed, before, weights, direct=None):
        size = weights.shape[0]
        width, rows, part = self.width, 2 * self.half, self.part
        shape = jax.ShapeDtypeStruct
        if direct is None:
            outs = [shape((rows, width), F32)]
        else:
            pairs, joined = self.groups // 2 - 1, width - direct
            outs = [shape((part, width), F32), shape((part, width + pairs * joined), BF16)]
            outs += [shape((part, direct), BF16)] * (2 * pairs) + [shape((part, joined), F32)] * pairs
        return self.call(
            functools.partial(down_kernel, not before, direct),
            [WHOLE] * (3 + len(before)),
            outs,
            [pltpu.VMEM((rows, size), BF16)],
            2 * rows * width * size,
            rows * size,
            6 * MIB,
            (*packed, *before, weights),
        )

    def __call__(self, tokens, gate_weight, up_weight, down_weight):
        self.gate_weight, self.up_weight, self.down_weight = (
            pltpu.with_memory_space_constraint(w, pltpu.HBM) for w in (gate_weight, up_weight, down_weight)
        )
        self.part, self.width = tokens.shape
        groups = self.groups
        self.half = self.part * groups // 2
        self.block = self.half // self.wide
        units = gate_weight.shape[1]
        step = units // 26 if units // 26 % 128 == 0 else units // 13
        count = units // step
        cuts = [count * c // 26 * step for c in (0, 9, 17, 26)]
        (s0, n0), (s1, n1), (s2, n2) = [(a, b - a) for a, b in zip(cuts[:-1], cuts[1:])]
        both = (NEAR_ROWS, FAR_ROWS)

        blocks = [tokens] + [self.along_z(tokens, j) for j in range(1, groups)]
        self.parts = (blocks[: groups // 2], blocks[groups // 2 :])

        w0 = self.fetch(s0, n0)
        w1 = self.fetch(s1, n1)
        a0, _ = self.held_gate_up(w0, None)
        a1, w2 = self.held_gate_up(w1, (s2, count * 4 // 26 * step))
        b0 = self.chip_sum(both, a0)
        a2 = self.gate_up(s2, n2, w2, 2)
        b1 = self.chip_sum(both, a1)
        h0 = self.hidden(b0)
        b2 = self.chip_sum(both, a2)
        d0 = self.fetch_rows(s0, n0)
        h1 = self.hidden(b1)
        d1 = self.fetch_rows(s1, n1)
        p0 = self.pack(h0)
        d2 = self.fetch_rows(s2, n2)
        h2 = self.hidden(b2)
        value = self.down(p0, [], d0)
        p1 = self.pack(h1)
        p2 = self.pack(h2)
        value = self.down(p1, value, d1)
        direct = self.width // 128 * 10 // 16 * 128
        own, soon, *late = self.down(p2, value, d2, direct)
        straight, held = late[: groups - 2], late[groups - 2 :]
        soon = self.along_z(soon, 1)
        straight = [self.along_z(v, 2 + j) for j, v in enumerate(straight)]
        size = self.width - direct
        joined = self.call(
            functools.partial(pair_sum_kernel, self.width),
            [WHOLE] * (1 + len(held)),
            [jax.ShapeDtypeStruct((self.part, size), BF16)] * len(held),
            [],
            256,
            1024,
            4 * MIB,
            (soon, *held),
        )
        joined = [self.along_z(v, 2 + 2 * j) for j, v in enumerate(joined)]
        (mixed,) = self.call(
            functools.partial(final_kernel, direct, groups - 2),
            [WHOLE] * (2 + len(straight) + len(joined)),
            [jax.ShapeDtypeStruct((self.part, self.width), BF16)],
            [],
            256,
            1024,
            4 * MIB,
            (own, soon, *straight, *joined),
        )
        return mixed


def solution(mesh):
    placed = (P(("group", "hid"), "wid"), P("wid", "hid"), P("wid", "hid"), P("hid", "wid"))

    def run(*arrays):
        return Body(mesh.shape["hid"], mesh.shape["wid"])(*arrays)

    return jax.shard_map(run, mesh=mesh, in_specs=placed, out_specs=P(("group", "hid"), "wid"), check_vma=False)
```

```python
import functools

import jax
import jax.numpy as jnp
from jax import lax
from jax.experimental import pallas as pl
from jax.experimental.pallas import tpu as pltpu
from jax.sharding import PartitionSpec as P

MIB = 1 << 20
F32, BF16 = jnp.float32, jnp.bfloat16
WHOLE = pl.BlockSpec(memory_space=pltpu.VMEM)
FAR = pl.BlockSpec(memory_space=pltpu.HBM)
STAY = pl.BlockSpec(memory_space=pl.ANY)
NEAR_ROWS, FAR_ROWS = 0, 1


def largest(total, options):
    return next(o for o in options if total % o == 0)


def fetch_start(copies):
    for copy in copies:
        copy.start()


def fetch_wait(copies):
    for copy in copies:
        copy.wait()


def column_copies(start, sources, targets, sems):
    pieces = sems.shape[0] // 2
    depth = targets[0].shape[0] // pieces
    copies = []
    for i in range(2 * pieces):
        at = pl.ds(i // 2 * depth, depth)
        source, target = sources[i % 2], targets[i % 2]
        copies.append(
            pltpu.make_async_copy(source.at[at, pl.ds(start, target.shape[1])], target.at[at, :], sems.at[i])
        )
    return copies


def fetch_kernel(start, gate_ref, up_ref, gate_out, up_out, sems):
    copies = column_copies(start, (gate_ref, up_ref), (gate_out, up_out), sems)
    fetch_start(copies)
    fetch_wait(copies)


def order_rows(parts, left):
    rows = parts[0][0].shape[0]
    half = len(parts[0]) * rows
    other = 1 - lax.rem(lax.axis_index("wid"), 2)
    for h, blocks in enumerate(parts):
        for j, block in enumerate(blocks):
            at = h * half + lax.rem(j * rows + other * (half // 2), half)
            left[pl.ds(pl.multiple_of(at, rows), rows), :] = block[...]


def put_sums(sums, halves, send_refs, keep_ref, column):
    for which, value in enumerate(sums):
        quarter = value.shape[0] // (2 * halves)
        columns = slice(column, column + value.shape[1])
        for h in range(halves):
            at = 2 * h * quarter
            send = send_refs[h % len(send_refs)]
            send[h // len(send_refs), which, :, columns] = value[at : at + quarter].astype(BF16)
            keep_ref[h, which, :, columns] = value[at + quarter : at + 2 * quarter]


def split_parts(refs, halves, blocks):
    return [refs[h * blocks : (h + 1) * blocks] for h in range(halves)], refs[halves * blocks :]


def held_gate_up_kernel(halves, blocks, pieces, ahead, *refs):
    parts, refs = split_parts(refs, halves, blocks)
    pairs, refs = [refs[2 * p : 2 * p + 2] for p in range(pieces)], refs[2 * pieces :]
    copies = []
    if ahead is not None:
        sources, refs, sems = refs[:2], refs[2:-1], refs[-1]
        copies = column_copies(ahead, sources, refs[2:4], sems)
        refs = refs[:2] + refs[4:]
    send_ref, keep_ref, left = refs
    fetch_start(copies)
    order_rows(parts, left)
    column = 0
    for pair in pairs:
        sums = [jnp.dot(left[...], w[...], preferred_element_type=F32) for w in pair]
        put_sums(sums, halves, [send_ref], keep_ref, column)
        column += pair[0].shape[1]
    fetch_wait(copies)


def gate_up_kernel(start, width, depth, slots, halves, blocks, sends, *refs):
    parts, refs = split_parts(refs, halves, blocks)
    held_refs, (gate_ref, up_ref), refs = refs[:2], refs[2:4], refs[4:]
    send_refs, keep_ref, left, held, sems = refs[:sends], *refs[sends:]
    before = held_refs[0].shape[1]
    total = 2 * (left.shape[1] // depth)

    def copy(i):
        source = (gate_ref, up_ref)[i % 2]
        slot = i % slots
        return pltpu.make_async_copy(
            source.at[pl.ds(i // 2 * depth, depth), pl.ds(start + before, width - before)], held.at[slot], sems.at[slot]
        )

    for i in range(min(slots, total)):
        copy(i).start()
    order_rows(parts, left)
    sums = [jnp.dot(left[...], w[...], preferred_element_type=F32) for w in held_refs]
    put_sums(sums, halves, send_refs, keep_ref, 0)
    sums = [None, None]
    for i in range(total):
        copy(i).wait()
        product = jnp.dot(left[:, pl.ds(i // 2 * depth, depth)], held[i % slots], preferred_element_type=F32)
        sums[i % 2] = product if i < 2 else sums[i % 2] + product
        if i + slots < total:
            copy(i + slots).start()
    put_sums(sums, halves, send_refs, keep_ref, before)


def chip_sum_kernel(chips, halves, keep, *refs):
    came, outs = refs[:-chips], refs[-chips:]
    rows = outs[0].shape[2]
    me = lax.axis_index("wid") // 2
    for j in range(chips):
        at = pl.ds(pl.multiple_of(lax.rem(me + j, chips) * rows, rows), rows)
        for h in range(halves):
            for which in range(2):
                other = came[h % len(came)][h // len(came), which, at, :]
                outs[j][h, which] = (keep[h, which, at, :] + other.astype(F32)).astype(outs[j].dtype)


def hidden_kernel(own_ref, *refs):
    came_refs, hidden_ref = refs[:-1], refs[-1]
    for h in range(own_ref.shape[0]):
        gate, up = own_ref[h, 0], own_ref[h, 1]
        for came in came_refs:
            gate = gate + came[h, 0].astype(F32)
            up = up + came[h, 1].astype(F32)
        hidden_ref[h] = (gate / (1.0 + jnp.exp(-gate)) * up).astype(BF16)


def pack_kernel(*refs):
    for j, ref in enumerate(refs[:-1]):
        refs[-1][j] = ref[...]


def fetch_rows_kernel(start, down_ref, out_ref, sems):
    pieces = sems.shape[0]
    rows = out_ref.shape[0] // pieces
    copies = [
        pltpu.make_async_copy(
            down_ref.at[pl.ds(start + p * rows, rows), :], out_ref.at[pl.ds(p * rows, rows), :], sems.at[p]
        )
        for p in range(pieces)
    ]
    fetch_start(copies)
    fetch_wait(copies)


def place_hidden(pairs, left):
    x, core = lax.axis_index("wid") // 2, lax.rem(lax.axis_index("wid"), 2)
    for side, ref in enumerate(pairs):
        chips, halves, rows, _ = ref.shape
        quarter = left.shape[0] // (2 * halves)
        for h in range(halves):
            for j in range(chips):
                base = (2 * h + (core if side == 0 else 1 - core)) * quarter
                at = base + lax.rem(x - j + chips, chips) * rows
                left[pl.ds(pl.multiple_of(at, rows), rows), :] = ref[j, h]


def down_kernel(first, direct, near_ref, far_ref, *refs):
    if not first:
        before_ref, refs = refs[0], refs[1:]
    down_ref, outs, left = refs[0], refs[1:-1], refs[-1]
    place_hidden((near_ref, far_ref), left)
    value = jnp.dot(left[...], down_ref[...], preferred_element_type=F32)
    if not first:
        value = value + before_ref[...]
    if direct is None:
        outs[0][...] = value
        return
    own_ref, soon_ref, *late_refs = outs
    rows, width = own_ref.shape
    blocks = value.shape[0] // rows
    straight, held = late_refs[: blocks - 2], late_refs[blocks - 2 :]
    own_ref[...] = value[:rows]
    soon_ref[:, :width] = value[rows : 2 * rows].astype(BF16)
    for j in range(2, blocks):
        block = value[j * rows : (j + 1) * rows]
        straight[j - 2][...] = block[:, :direct].astype(BF16)
        if j % 2 == 0:
            held[j // 2 - 1][...] = block[:, direct:]
        else:
            at = width + (j // 2 - 1) * (width - direct)
            soon_ref[:, at : at + width - direct] = block[:, direct:].astype(BF16)


def pair_sum_kernel(width, soon_ref, *refs):
    count = len(refs) // 2
    for held, out in zip(refs[:count], refs[count:]):
        size = held.shape[1]
        out[...] = (held[...] + soon_ref[:, width : width + size].astype(F32)).astype(BF16)
        width += size


def final_kernel(direct, count, own_ref, soon_ref, *refs):
    straight, joined, out_ref = refs[:count], refs[count:-1], refs[-1]
    width = own_ref.shape[1]
    value = own_ref[...] + soon_ref[:, :width].astype(F32)
    for side, arrays in ((slice(0, direct), straight), (slice(direct, width), joined)):
        part = value[:, side]
        for came in arrays:
            part = part + came[...].astype(F32)
        out_ref[:, side] = part.astype(out_ref.dtype)


class Body:
    def __init__(self, groups, wide):
        self.groups, self.wide, self.chips = groups, wide, wide // 2
        self.last = None

    def call(self, kernel, ins, outs, scratch, flops, moved, limit, args):
        after = [] if self.last is None else [self.last]

        def run(*refs):
            kernel(*refs[len(after) :])

        got = pl.pallas_call(
            run,
            name=kernel.func.__name__ if isinstance(kernel, functools.partial) else kernel.__name__,
            in_specs=[STAY] * len(after) + ins,
            out_specs=[WHOLE] * len(outs),
            out_shape=outs,
            scratch_shapes=scratch,
            compiler_params=pltpu.CompilerParams(vmem_limit_bytes=limit),
            cost_estimate=pl.CostEstimate(flops=flops, bytes_accessed=moved, transcendentals=0),
        )(*after, *args)
        self.last = got[0]
        return got

    def other_core(self, value):
        return lax.ppermute(value, "wid", [(w, w ^ 1) for w in range(self.wide)])

    def along_x(self, value, j):
        return lax.ppermute(value, "wid", [(w, (w // 2 + j) % self.chips * 2 + w % 2) for w in range(self.wide)])

    def along_z(self, value, j):
        return lax.ppermute(value, "hid", [(z, z ^ j) for z in range(self.groups)])

    def gate_up_parts(self):
        parts = [p for h in self.parts for p in h]
        return parts, len(parts) * self.part

    def held_gate_up(self, pairs, ahead):
        weights = [w for pair in pairs for w in pair]
        parts, rows = self.gate_up_parts()
        size = sum(w.shape[1] for w in weights) // 2
        outs = [jax.ShapeDtypeStruct((2, 2, rows // 4, size), t) for t in (BF16, F32)]
        ins, more = [WHOLE] * (len(parts) + len(weights)), ()
        scratch = [pltpu.VMEM((rows, self.width), BF16)]
        if ahead is not None:
            outs += [jax.ShapeDtypeStruct((self.width, ahead[1]), BF16)] * 2
            ins, more = ins + [FAR] * 2, (self.gate_weight, self.up_weight)
            scratch.append(pltpu.SemaphoreType.DMA((2,)))
        got = self.call(
            functools.partial(held_gate_up_kernel, 2, self.groups // 2, len(pairs), None if ahead is None else ahead[0]),
            ins,
            outs,
            scratch,
            4 * rows * self.width * size,
            rows * self.width,
            6 * MIB,
            (*parts, *weights, *more),
        )
        return (got[1], self.other_core(got[0])), got[2:]

    def gate_up(self, start, size, weights, sends):
        parts, rows = self.gate_up_parts()
        width = self.width
        outs = [jax.ShapeDtypeStruct((2 // sends, 2, rows // 4, size), BF16)] * sends
        outs.append(jax.ShapeDtypeStruct((2, 2, rows // 4, size), F32))
        depth, slots = largest(width, (512, 256)), 8
        streamed = size - weights[0].shape[1]
        got = self.call(
            functools.partial(gate_up_kernel, start, size, depth, slots, 2, self.groups // 2, sends),
            [WHOLE] * (len(parts) + 2) + [FAR] * 2,
            outs,
            [
                pltpu.VMEM((rows, width), BF16),
                pltpu.VMEM((slots, depth, streamed), BF16),
                pltpu.SemaphoreType.DMA((slots,)),
            ],
            4 * rows * width * size,
            4 * width * size,
            26 * MIB,
            (*parts, *weights, self.gate_weight, self.up_weight),
        )
        return got[-1], *(self.other_core(v) for v in got[:-1])

    def fetch(self, start, size):
        return self.call(
            functools.partial(fetch_kernel, start),
            [FAR] * 2,
            [jax.ShapeDtypeStruct((self.width, size), BF16)] * 2,
            [pltpu.SemaphoreType.DMA((2,))],
            0,
            4 * self.width * size,
            2 * MIB,
            (self.gate_weight, self.up_weight),
        )

    def chip_sum(self, halves, args):
        size = args[0].shape[3]
        block = (len(halves), 2, self.block, size)
        own, *sends = self.call(
            functools.partial(chip_sum_kernel, self.chips, len(halves)),
            [WHOLE] * len(args),
            [jax.ShapeDtypeStruct(block, F32)] + [jax.ShapeDtypeStruct(block, BF16)] * (self.chips - 1),
            [],
            size * 256,
            size * 1024,
            4 * MIB,
            args,
        )
        return own, [self.along_x(v, j + 1) for j, v in enumerate(sends)]

    def hidden(self, summed):
        own, came = summed
        n, _, rows, size = own.shape
        (mine,) = self.call(
            hidden_kernel,
            [WHOLE] * (1 + len(came)),
            [jax.ShapeDtypeStruct((n, rows, size), BF16)],
            [],
            size * 256,
            size * 1024,
            4 * MIB,
            (own, *came),
        )
        return [mine] + [self.along_x(mine, j) for j in range(1, self.chips)]

    def pack(self, near):
        shape = jax.ShapeDtypeStruct((len(near),) + near[0].shape, BF16)
        (packed,) = self.call(pack_kernel, [WHOLE] * len(near), [shape], [], 256, 1024, 4 * MIB, near)
        return packed, self.other_core(packed)

    def fetch_rows(self, start, size):
        (rows,) = self.call(
            functools.partial(fetch_rows_kernel, start),
            [FAR],
            [jax.ShapeDtypeStruct((size, self.width), BF16)],
            [pltpu.SemaphoreType.DMA((1,))],
            0,
            2 * self.width * size,
            2 * MIB,
            (self.down_weight,),
        )
        return rows

    def down(self, packed, before, weights, direct=None):
        size = weights.shape[0]
        width, rows, part = self.width, 2 * self.half, self.part
        shape = jax.ShapeDtypeStruct
        if direct is None:
            outs = [shape((rows, width), F32)]
        else:
            pairs, joined = self.groups // 2 - 1, width - direct
            outs = [shape((part, width), F32), shape((part, width + pairs * joined), BF16)]
            outs += [shape((part, direct), BF16)] * (2 * pairs) + [shape((part, joined), F32)] * pairs
        return self.call(
            functools.partial(down_kernel, not before, direct),
            [WHOLE] * (3 + len(before)),
            outs,
            [pltpu.VMEM((rows, size), BF16)],
            2 * rows * width * size,
            rows * size,
            6 * MIB,
            (*packed, *before, weights),
        )

    def __call__(self, tokens, gate_weight, up_weight, down_weight):
        self.gate_weight, self.up_weight, self.down_weight = (
            pltpu.with_memory_space_constraint(w, pltpu.HBM) for w in (gate_weight, up_weight, down_weight)
        )
        self.part, self.width = tokens.shape
        groups = self.groups
        self.half = self.part * groups // 2
        self.block = self.half // self.wide
        units = gate_weight.shape[1]
        step = units // 26 if units // 26 % 128 == 0 else units // 13
        count = units // step
        cuts = [count * c // 26 * step for c in (0, 9, 17, 26)]
        (s0, n0), (s1, n1), (s2, n2) = [(a, b - a) for a, b in zip(cuts[:-1], cuts[1:])]
        both = (NEAR_ROWS, FAR_ROWS)

        blocks = [tokens] + [self.along_z(tokens, j) for j in range(1, groups)]
        self.parts = (blocks[: groups // 2], blocks[groups // 2 :])

        part = count * 6 // 26 * step
        w0 = self.fetch(s0, n0)
        w1 = self.fetch(s1, part)
        a0, rest = self.held_gate_up([w0], (s1 + part, n1 - part))
        a1, w2 = self.held_gate_up([w1, rest], (s2, count * 2 // 26 * step))
        b0 = self.chip_sum(both, a0)
        a2 = self.gate_up(s2, n2, w2, 2)
        b1 = self.chip_sum(both, a1)
        h0 = self.hidden(b0)
        b2 = self.chip_sum(both, a2)
        d0 = self.fetch_rows(s0, n0)
        h1 = self.hidden(b1)
        d1 = self.fetch_rows(s1, n1)
        p0 = self.pack(h0)
        d2 = self.fetch_rows(s2, n2)
        h2 = self.hidden(b2)
        value = self.down(p0, [], d0)
        p1 = self.pack(h1)
        p2 = self.pack(h2)
        value = self.down(p1, value, d1)
        direct = self.width // 128 * 10 // 16 * 128
        own, soon, *late = self.down(p2, value, d2, direct)
        straight, held = late[: groups - 2], late[groups - 2 :]
        soon = self.along_z(soon, 1)
        straight = [self.along_z(v, 2 + j) for j, v in enumerate(straight)]
        size = self.width - direct
        joined = self.call(
            functools.partial(pair_sum_kernel, self.width),
            [WHOLE] * (1 + len(held)),
            [jax.ShapeDtypeStruct((self.part, size), BF16)] * len(held),
            [],
            256,
            1024,
            4 * MIB,
            (soon, *held),
        )
        joined = [self.along_z(v, 2 + 2 * j) for j, v in enumerate(joined)]
        (mixed,) = self.call(
            functools.partial(final_kernel, direct, groups - 2),
            [WHOLE] * (2 + len(straight) + len(joined)),
            [jax.ShapeDtypeStruct((self.part, self.width), BF16)],
            [],
            256,
            1024,
            4 * MIB,
            (own, soon, *straight, *joined),
        )
        return mixed


def solution(mesh):
    placed = (P(("group", "hid"), "wid"), P("wid", "hid"), P("wid", "hid"), P("hid", "wid"))

    def run(*arrays):
        return Body(mesh.shape["hid"], mesh.shape["wid"])(*arrays)

    return jax.shard_map(run, mesh=mesh, in_specs=placed, out_specs=P(("group", "hid"), "wid"), check_vma=False)
```

```python
import functools

import jax
import jax.numpy as jnp
from jax import lax
from jax.experimental import pallas as pl
from jax.experimental.pallas import tpu as pltpu
from jax.sharding import PartitionSpec as P

MIB = 1 << 20
F32, BF16 = jnp.float32, jnp.bfloat16
WHOLE = pl.BlockSpec(memory_space=pltpu.VMEM)
FAR = pl.BlockSpec(memory_space=pltpu.HBM)
STAY = pl.BlockSpec(memory_space=pl.ANY)
NEAR_ROWS, FAR_ROWS = 0, 1


def largest(total, options):
    return next(o for o in options if total % o == 0)


def fetch_start(copies):
    for copy in copies:
        copy.start()


def fetch_wait(copies):
    for copy in copies:
        copy.wait()


def column_copies(start, sources, targets, sems):
    pieces = sems.shape[0] // 2
    depth = targets[0].shape[0] // pieces
    copies = []
    for i in range(2 * pieces):
        at = pl.ds(i // 2 * depth, depth)
        source, target = sources[i % 2], targets[i % 2]
        copies.append(
            pltpu.make_async_copy(source.at[at, pl.ds(start, target.shape[1])], target.at[at, :], sems.at[i])
        )
    return copies


def fetch_kernel(start, gate_ref, up_ref, gate_out, up_out, sems):
    copies = column_copies(start, (gate_ref, up_ref), (gate_out, up_out), sems)
    fetch_start(copies)
    fetch_wait(copies)


def order_rows(parts, left):
    rows = parts[0][0].shape[0]
    half = len(parts[0]) * rows
    other = 1 - lax.rem(lax.axis_index("wid"), 2)
    for h, blocks in enumerate(parts):
        for j, block in enumerate(blocks):
            at = h * half + lax.rem(j * rows + other * (half // 2), half)
            left[pl.ds(pl.multiple_of(at, rows), rows), :] = block[...]


def put_sums(sums, halves, send_refs, keep_ref, column):
    for which, value in enumerate(sums):
        quarter = value.shape[0] // (2 * halves)
        columns = slice(column, column + value.shape[1])
        for h in range(halves):
            at = 2 * h * quarter
            send = send_refs[h % len(send_refs)]
            send[h // len(send_refs), which, :, columns] = value[at : at + quarter].astype(BF16)
            keep_ref[h, which, :, columns] = value[at + quarter : at + 2 * quarter]


def split_parts(refs, halves, blocks):
    return [refs[h * blocks : (h + 1) * blocks] for h in range(halves)], refs[halves * blocks :]


def held_gate_up_kernel(halves, blocks, pieces, ahead, *refs):
    parts, refs = split_parts(refs, halves, blocks)
    pairs, refs = [refs[2 * p : 2 * p + 2] for p in range(pieces)], refs[2 * pieces :]
    copies = []
    if ahead is not None:
        sources, refs, sems = refs[:2], refs[2:-1], refs[-1]
        copies = column_copies(ahead, sources, refs[2:4], sems)
        refs = refs[:2] + refs[4:]
    send_ref, keep_ref, left = refs
    fetch_start(copies)
    order_rows(parts, left)
    column = 0
    for pair in pairs:
        sums = [jnp.dot(left[...], w[...], preferred_element_type=F32) for w in pair]
        put_sums(sums, halves, [send_ref], keep_ref, column)
        column += pair[0].shape[1]
    fetch_wait(copies)


def gate_up_kernel(start, width, depth, slots, halves, blocks, sends, *refs):
    parts, refs = split_parts(refs, halves, blocks)
    held_refs, (gate_ref, up_ref), refs = refs[:2], refs[2:4], refs[4:]
    send_refs, keep_ref, left, held, sems = refs[:sends], *refs[sends:]
    before = held_refs[0].shape[1]
    total = 2 * (left.shape[1] // depth)

    def copy(i):
        source = (gate_ref, up_ref)[i % 2]
        slot = i % slots
        return pltpu.make_async_copy(
            source.at[pl.ds(i // 2 * depth, depth), pl.ds(start + before, width - before)], held.at[slot], sems.at[slot]
        )

    for i in range(min(slots, total)):
        copy(i).start()
    order_rows(parts, left)
    sums = [jnp.dot(left[...], w[...], preferred_element_type=F32) for w in held_refs]
    put_sums(sums, halves, send_refs, keep_ref, 0)
    sums = [None, None]
    for i in range(total):
        copy(i).wait()
        product = jnp.dot(left[:, pl.ds(i // 2 * depth, depth)], held[i % slots], preferred_element_type=F32)
        sums[i % 2] = product if i < 2 else sums[i % 2] + product
        if i + slots < total:
            copy(i + slots).start()
    put_sums(sums, halves, send_refs, keep_ref, before)


def chip_sum_kernel(chips, halves, keep, *refs):
    came, outs = refs[:-chips], refs[-chips:]
    rows = outs[0].shape[2]
    me = lax.axis_index("wid") // 2
    for j in range(chips):
        at = pl.ds(pl.multiple_of(lax.rem(me + j, chips) * rows, rows), rows)
        for h in range(halves):
            for which in range(2):
                other = came[h % len(came)][h // len(came), which, at, :]
                outs[j][h, which] = (keep[h, which, at, :] + other.astype(F32)).astype(outs[j].dtype)


def hidden_kernel(own_ref, *refs):
    came_refs, hidden_ref = refs[:-1], refs[-1]
    for h in range(own_ref.shape[0]):
        gate, up = own_ref[h, 0], own_ref[h, 1]
        for came in came_refs:
            gate = gate + came[h, 0].astype(F32)
            up = up + came[h, 1].astype(F32)
        hidden_ref[h] = (gate / (1.0 + jnp.exp(-gate)) * up).astype(BF16)


def pack_kernel(*refs):
    for j, ref in enumerate(refs[:-1]):
        refs[-1][j] = ref[...]


def fetch_rows_kernel(start, down_ref, out_ref, sems):
    pieces = sems.shape[0]
    rows = out_ref.shape[0] // pieces
    copies = [
        pltpu.make_async_copy(
            down_ref.at[pl.ds(start + p * rows, rows), :], out_ref.at[pl.ds(p * rows, rows), :], sems.at[p]
        )
        for p in range(pieces)
    ]
    fetch_start(copies)
    fetch_wait(copies)


def place_hidden(pairs, left):
    x, core = lax.axis_index("wid") // 2, lax.rem(lax.axis_index("wid"), 2)
    for side, ref in enumerate(pairs):
        chips, halves, rows, _ = ref.shape
        quarter = left.shape[0] // (2 * halves)
        for h in range(halves):
            for j in range(chips):
                base = (2 * h + (core if side == 0 else 1 - core)) * quarter
                at = base + lax.rem(x - j + chips, chips) * rows
                left[pl.ds(pl.multiple_of(at, rows), rows), :] = ref[j, h]


def down_kernel(first, direct, near_ref, far_ref, *refs):
    if not first:
        before_ref, refs = refs[0], refs[1:]
    down_ref, outs, left = refs[0], refs[1:-1], refs[-1]
    place_hidden((near_ref, far_ref), left)
    value = jnp.dot(left[...], down_ref[...], preferred_element_type=F32)
    if not first:
        value = value + before_ref[...]
    if direct is None:
        outs[0][...] = value
        return
    own_ref, soon_ref, *late_refs = outs
    rows, width = own_ref.shape
    blocks = value.shape[0] // rows
    straight, held = late_refs[: blocks - 2], late_refs[blocks - 2 :]
    own_ref[...] = value[:rows]
    soon_ref[:, :width] = value[rows : 2 * rows].astype(BF16)
    for j in range(2, blocks):
        block = value[j * rows : (j + 1) * rows]
        straight[j - 2][...] = block[:, :direct].astype(BF16)
        if j % 2 == 0:
            held[j // 2 - 1][...] = block[:, direct:]
        else:
            at = width + (j // 2 - 1) * (width - direct)
            soon_ref[:, at : at + width - direct] = block[:, direct:].astype(BF16)


def pair_sum_kernel(width, soon_ref, *refs):
    count = len(refs) // 2
    for held, out in zip(refs[:count], refs[count:]):
        size = held.shape[1]
        out[...] = (held[...] + soon_ref[:, width : width + size].astype(F32)).astype(BF16)
        width += size


def final_kernel(direct, count, own_ref, soon_ref, *refs):
    straight, joined, out_ref = refs[:count], refs[count:-1], refs[-1]
    width = own_ref.shape[1]
    value = own_ref[...] + soon_ref[:, :width].astype(F32)
    for side, arrays in ((slice(0, direct), straight), (slice(direct, width), joined)):
        part = value[:, side]
        for came in arrays:
            part = part + came[...].astype(F32)
        out_ref[:, side] = part.astype(out_ref.dtype)


class Body:
    def __init__(self, groups, wide):
        self.groups, self.wide, self.chips = groups, wide, wide // 2
        self.last = None

    def call(self, kernel, ins, outs, scratch, flops, moved, limit, args):
        after = [] if self.last is None else [self.last]

        def run(*refs):
            kernel(*refs[len(after) :])

        got = pl.pallas_call(
            run,
            name=kernel.func.__name__ if isinstance(kernel, functools.partial) else kernel.__name__,
            in_specs=[STAY] * len(after) + ins,
            out_specs=[WHOLE] * len(outs),
            out_shape=outs,
            scratch_shapes=scratch,
            compiler_params=pltpu.CompilerParams(vmem_limit_bytes=limit),
            cost_estimate=pl.CostEstimate(flops=flops, bytes_accessed=moved, transcendentals=0),
        )(*after, *args)
        self.last = got[0]
        return got

    def other_core(self, value):
        return lax.ppermute(value, "wid", [(w, w ^ 1) for w in range(self.wide)])

    def along_x(self, value, j):
        return lax.ppermute(value, "wid", [(w, (w // 2 + j) % self.chips * 2 + w % 2) for w in range(self.wide)])

    def along_z(self, value, j):
        return lax.ppermute(value, "hid", [(z, z ^ j) for z in range(self.groups)])

    def gate_up_parts(self):
        parts = [p for h in self.parts for p in h]
        return parts, len(parts) * self.part

    def held_gate_up(self, pairs, ahead):
        weights = [w for pair in pairs for w in pair]
        parts, rows = self.gate_up_parts()
        size = sum(w.shape[1] for w in weights) // 2
        outs = [jax.ShapeDtypeStruct((2, 2, rows // 4, size), t) for t in (BF16, F32)]
        ins, more = [WHOLE] * (len(parts) + len(weights)), ()
        scratch = [pltpu.VMEM((rows, self.width), BF16)]
        if ahead is not None:
            outs += [jax.ShapeDtypeStruct((self.width, ahead[1]), BF16)] * 2
            ins, more = ins + [FAR] * 2, (self.gate_weight, self.up_weight)
            scratch.append(pltpu.SemaphoreType.DMA((2,)))
        got = self.call(
            functools.partial(held_gate_up_kernel, 2, self.groups // 2, len(pairs), None if ahead is None else ahead[0]),
            ins,
            outs,
            scratch,
            4 * rows * self.width * size,
            rows * self.width,
            6 * MIB,
            (*parts, *weights, *more),
        )
        return (got[1], self.other_core(got[0])), got[2:]

    def gate_up(self, start, size, weights, sends):
        parts, rows = self.gate_up_parts()
        width = self.width
        outs = [jax.ShapeDtypeStruct((2 // sends, 2, rows // 4, size), BF16)] * sends
        outs.append(jax.ShapeDtypeStruct((2, 2, rows // 4, size), F32))
        depth, slots = largest(width, (256, 128)), 16
        streamed = size - weights[0].shape[1]
        got = self.call(
            functools.partial(gate_up_kernel, start, size, depth, slots, 2, self.groups // 2, sends),
            [WHOLE] * (len(parts) + 2) + [FAR] * 2,
            outs,
            [
                pltpu.VMEM((rows, width), BF16),
                pltpu.VMEM((slots, depth, streamed), BF16),
                pltpu.SemaphoreType.DMA((slots,)),
            ],
            4 * rows * width * size,
            4 * width * size,
            26 * MIB,
            (*parts, *weights, self.gate_weight, self.up_weight),
        )
        return got[-1], *(self.other_core(v) for v in got[:-1])

    def fetch(self, start, size):
        return self.call(
            functools.partial(fetch_kernel, start),
            [FAR] * 2,
            [jax.ShapeDtypeStruct((self.width, size), BF16)] * 2,
            [pltpu.SemaphoreType.DMA((2,))],
            0,
            4 * self.width * size,
            2 * MIB,
            (self.gate_weight, self.up_weight),
        )

    def chip_sum(self, halves, args):
        size = args[0].shape[3]
        block = (len(halves), 2, self.block, size)
        own, *sends = self.call(
            functools.partial(chip_sum_kernel, self.chips, len(halves)),
            [WHOLE] * len(args),
            [jax.ShapeDtypeStruct(block, F32)] + [jax.ShapeDtypeStruct(block, BF16)] * (self.chips - 1),
            [],
            size * 256,
            size * 1024,
            4 * MIB,
            args,
        )
        return own, [self.along_x(v, j + 1) for j, v in enumerate(sends)]

    def hidden(self, summed):
        own, came = summed
        n, _, rows, size = own.shape
        (mine,) = self.call(
            hidden_kernel,
            [WHOLE] * (1 + len(came)),
            [jax.ShapeDtypeStruct((n, rows, size), BF16)],
            [],
            size * 256,
            size * 1024,
            4 * MIB,
            (own, *came),
        )
        return [mine] + [self.along_x(mine, j) for j in range(1, self.chips)]

    def pack(self, near):
        shape = jax.ShapeDtypeStruct((len(near),) + near[0].shape, BF16)
        (packed,) = self.call(pack_kernel, [WHOLE] * len(near), [shape], [], 256, 1024, 4 * MIB, near)
        return packed, self.other_core(packed)

    def fetch_rows(self, start, size):
        (rows,) = self.call(
            functools.partial(fetch_rows_kernel, start),
            [FAR],
            [jax.ShapeDtypeStruct((size, self.width), BF16)],
            [pltpu.SemaphoreType.DMA((1,))],
            0,
            2 * self.width * size,
            2 * MIB,
            (self.down_weight,),
        )
        return rows

    def down(self, packed, before, weights, direct=None):
        size = weights.shape[0]
        width, rows, part = self.width, 2 * self.half, self.part
        shape = jax.ShapeDtypeStruct
        if direct is None:
            outs = [shape((rows, width), F32)]
        else:
            pairs, joined = self.groups // 2 - 1, width - direct
            outs = [shape((part, width), F32), shape((part, width + pairs * joined), BF16)]
            outs += [shape((part, direct), BF16)] * (2 * pairs) + [shape((part, joined), F32)] * pairs
        return self.call(
            functools.partial(down_kernel, not before, direct),
            [WHOLE] * (3 + len(before)),
            outs,
            [pltpu.VMEM((rows, size), BF16)],
            2 * rows * width * size,
            rows * size,
            6 * MIB,
            (*packed, *before, weights),
        )

    def __call__(self, tokens, gate_weight, up_weight, down_weight):
        self.gate_weight, self.up_weight, self.down_weight = (
            pltpu.with_memory_space_constraint(w, pltpu.HBM) for w in (gate_weight, up_weight, down_weight)
        )
        self.part, self.width = tokens.shape
        groups = self.groups
        self.half = self.part * groups // 2
        self.block = self.half // self.wide
        units = gate_weight.shape[1]
        step = units // 26 if units // 26 % 128 == 0 else units // 13
        count = units // step
        cuts = [count * c // 26 * step for c in (0, 9, 17, 26)]
        (s0, n0), (s1, n1), (s2, n2) = [(a, b - a) for a, b in zip(cuts[:-1], cuts[1:])]
        both = (NEAR_ROWS, FAR_ROWS)

        blocks = [tokens] + [self.along_z(tokens, j) for j in range(1, groups)]
        self.parts = (blocks[: groups // 2], blocks[groups // 2 :])

        part = count * 6 // 26 * step
        w0 = self.fetch(s0, n0)
        w1 = self.fetch(s1, part)
        a0, rest = self.held_gate_up([w0], (s1 + part, n1 - part))
        a1, w2 = self.held_gate_up([w1, rest], (s2, count * 2 // 26 * step))
        b0 = self.chip_sum(both, a0)
        a2 = self.gate_up(s2, n2, w2, 2)
        b1 = self.chip_sum(both, a1)
        h0 = self.hidden(b0)
        b2 = self.chip_sum(both, a2)
        d0 = self.fetch_rows(s0, n0)
        h1 = self.hidden(b1)
        d1 = self.fetch_rows(s1, n1)
        p0 = self.pack(h0)
        d2 = self.fetch_rows(s2, n2)
        h2 = self.hidden(b2)
        value = self.down(p0, [], d0)
        p1 = self.pack(h1)
        p2 = self.pack(h2)
        value = self.down(p1, value, d1)
        direct = self.width // 128 * 10 // 16 * 128
        own, soon, *late = self.down(p2, value, d2, direct)
        straight, held = late[: groups - 2], late[groups - 2 :]
        soon = self.along_z(soon, 1)
        straight = [self.along_z(v, 2 + j) for j, v in enumerate(straight)]
        size = self.width - direct
        joined = self.call(
            functools.partial(pair_sum_kernel, self.width),
            [WHOLE] * (1 + len(held)),
            [jax.ShapeDtypeStruct((self.part, size), BF16)] * len(held),
            [],
            256,
            1024,
            4 * MIB,
            (soon, *held),
        )
        joined = [self.along_z(v, 2 + 2 * j) for j, v in enumerate(joined)]
        (mixed,) = self.call(
            functools.partial(final_kernel, direct, groups - 2),
            [WHOLE] * (2 + len(straight) + len(joined)),
            [jax.ShapeDtypeStruct((self.part, self.width), BF16)],
            [],
            256,
            1024,
            4 * MIB,
            (own, soon, *straight, *joined),
        )
        return mixed


def solution(mesh):
    placed = (P(("group", "hid"), "wid"), P("wid", "hid"), P("wid", "hid"), P("hid", "wid"))

    def run(*arrays):
        return Body(mesh.shape["hid"], mesh.shape["wid"])(*arrays)

    return jax.shard_map(run, mesh=mesh, in_specs=placed, out_specs=P(("group", "hid"), "wid"), check_vma=False)
```

```python
import functools

import jax
import jax.numpy as jnp
from jax import lax
from jax.experimental import pallas as pl
from jax.experimental.pallas import tpu as pltpu
from jax.sharding import PartitionSpec as P

MIB = 1 << 20
F32, BF16 = jnp.float32, jnp.bfloat16
WHOLE = pl.BlockSpec(memory_space=pltpu.VMEM)
FAR = pl.BlockSpec(memory_space=pltpu.HBM)
STAY = pl.BlockSpec(memory_space=pl.ANY)
NEAR_ROWS, FAR_ROWS = 0, 1


def largest(total, options):
    return next(o for o in options if total % o == 0)


def fetch_start(copies):
    for copy in copies:
        copy.start()


def fetch_wait(copies):
    for copy in copies:
        copy.wait()


def column_copies(start, sources, targets, sems):
    pieces = sems.shape[0] // 2
    depth = targets[0].shape[0] // pieces
    copies = []
    for i in range(2 * pieces):
        at = pl.ds(i // 2 * depth, depth)
        source, target = sources[i % 2], targets[i % 2]
        copies.append(
            pltpu.make_async_copy(source.at[at, pl.ds(start, target.shape[1])], target.at[at, :], sems.at[i])
        )
    return copies


def fetch_kernel(start, gate_ref, up_ref, gate_out, up_out, sems):
    copies = column_copies(start, (gate_ref, up_ref), (gate_out, up_out), sems)
    fetch_start(copies)
    fetch_wait(copies)


def order_rows(parts, left):
    rows = parts[0][0].shape[0]
    half = len(parts[0]) * rows
    other = 1 - lax.rem(lax.axis_index("wid"), 2)
    for h, blocks in enumerate(parts):
        for j, block in enumerate(blocks):
            at = h * half + lax.rem(j * rows + other * (half // 2), half)
            left[pl.ds(pl.multiple_of(at, rows), rows), :] = block[...]


def put_sums(sums, halves, send_refs, keep_ref, column):
    for which, value in enumerate(sums):
        quarter = value.shape[0] // (2 * halves)
        columns = slice(column, column + value.shape[1])
        for h in range(halves):
            at = 2 * h * quarter
            send = send_refs[h % len(send_refs)]
            send[h // len(send_refs), which, :, columns] = value[at : at + quarter].astype(BF16)
            keep_ref[h, which, :, columns] = value[at + quarter : at + 2 * quarter]


def split_parts(refs, halves, blocks):
    return [refs[h * blocks : (h + 1) * blocks] for h in range(halves)], refs[halves * blocks :]


def held_gate_up_kernel(halves, blocks, pieces, ahead, *refs):
    parts, refs = split_parts(refs, halves, blocks)
    pairs, refs = [refs[2 * p : 2 * p + 2] for p in range(pieces)], refs[2 * pieces :]
    copies = []
    if ahead is not None:
        sources, refs, sems = refs[:2], refs[2:-1], refs[-1]
        copies = column_copies(ahead, sources, refs[2:4], sems)
        refs = refs[:2] + refs[4:]
    send_ref, keep_ref, left = refs
    fetch_start(copies)
    order_rows(parts, left)
    column = 0
    for pair in pairs:
        sums = [jnp.dot(left[...], w[...], preferred_element_type=F32) for w in pair]
        put_sums(sums, halves, [send_ref], keep_ref, column)
        column += pair[0].shape[1]
    fetch_wait(copies)


def gate_up_kernel(start, width, depth, slots, halves, blocks, sends, *refs):
    parts, refs = split_parts(refs, halves, blocks)
    held_refs, (gate_ref, up_ref), refs = refs[:2], refs[2:4], refs[4:]
    send_refs, keep_ref, left, held, sems = refs[:sends], *refs[sends:]
    before = held_refs[0].shape[1]
    total = 2 * (left.shape[1] // depth)

    def copy(i):
        source = (gate_ref, up_ref)[i % 2]
        slot = i % slots
        return pltpu.make_async_copy(
            source.at[pl.ds(i // 2 * depth, depth), pl.ds(start + before, width - before)], held.at[slot], sems.at[slot]
        )

    for i in range(min(slots, total)):
        copy(i).start()
    order_rows(parts, left)
    sums = [jnp.dot(left[...], w[...], preferred_element_type=F32) for w in held_refs]
    put_sums(sums, halves, send_refs, keep_ref, 0)
    sums = [None, None]
    for i in range(total):
        copy(i).wait()
        product = jnp.dot(left[:, pl.ds(i // 2 * depth, depth)], held[i % slots], preferred_element_type=F32)
        sums[i % 2] = product if i < 2 else sums[i % 2] + product
        if i + slots < total:
            copy(i + slots).start()
    put_sums(sums, halves, send_refs, keep_ref, before)


def chip_sum_kernel(chips, halves, keep, *refs):
    came, outs = refs[:-chips], refs[-chips:]
    rows = outs[0].shape[2]
    me = lax.axis_index("wid") // 2
    for j in range(chips):
        at = pl.ds(pl.multiple_of(lax.rem(me + j, chips) * rows, rows), rows)
        for h in range(halves):
            for which in range(2):
                other = came[h % len(came)][h // len(came), which, at, :]
                outs[j][h, which] = (keep[h, which, at, :] + other.astype(F32)).astype(outs[j].dtype)


def hidden_kernel(own_ref, *refs):
    came_refs, hidden_ref = refs[:-1], refs[-1]
    for h in range(own_ref.shape[0]):
        gate, up = own_ref[h, 0], own_ref[h, 1]
        for came in came_refs:
            gate = gate + came[h, 0].astype(F32)
            up = up + came[h, 1].astype(F32)
        hidden_ref[h] = (gate / (1.0 + jnp.exp(-gate)) * up).astype(BF16)


def pack_kernel(*refs):
    for j, ref in enumerate(refs[:-1]):
        refs[-1][j] = ref[...]


def fetch_rows_kernel(start, down_ref, out_ref, sems):
    pieces = sems.shape[0]
    rows = out_ref.shape[0] // pieces
    copies = [
        pltpu.make_async_copy(
            down_ref.at[pl.ds(start + p * rows, rows), :], out_ref.at[pl.ds(p * rows, rows), :], sems.at[p]
        )
        for p in range(pieces)
    ]
    fetch_start(copies)
    fetch_wait(copies)


def place_hidden(pairs, left):
    x, core = lax.axis_index("wid") // 2, lax.rem(lax.axis_index("wid"), 2)
    for side, ref in enumerate(pairs):
        chips, halves, rows, _ = ref.shape
        quarter = left.shape[0] // (2 * halves)
        for h in range(halves):
            for j in range(chips):
                base = (2 * h + (core if side == 0 else 1 - core)) * quarter
                at = base + lax.rem(x - j + chips, chips) * rows
                left[pl.ds(pl.multiple_of(at, rows), rows), :] = ref[j, h]


def down_kernel(first, direct, near_ref, far_ref, *refs):
    if not first:
        before_ref, refs = refs[0], refs[1:]
    down_ref, outs, left = refs[0], refs[1:-1], refs[-1]
    place_hidden((near_ref, far_ref), left)
    value = jnp.dot(left[...], down_ref[...], preferred_element_type=F32)
    if not first:
        value = value + before_ref[...]
    if direct is None:
        outs[0][...] = value
        return
    own_ref, soon_ref, *late_refs = outs
    rows, width = own_ref.shape
    blocks = value.shape[0] // rows
    straight, held = late_refs[: blocks - 2], late_refs[blocks - 2 :]
    own_ref[...] = value[:rows]
    soon_ref[:, :width] = value[rows : 2 * rows].astype(BF16)
    for j in range(2, blocks):
        block = value[j * rows : (j + 1) * rows]
        straight[j - 2][...] = block[:, :direct].astype(BF16)
        if j % 2 == 0:
            held[j // 2 - 1][...] = block[:, direct:]
        else:
            at = width + (j // 2 - 1) * (width - direct)
            soon_ref[:, at : at + width - direct] = block[:, direct:].astype(BF16)


def pair_sum_kernel(width, soon_ref, *refs):
    count = len(refs) // 2
    for held, out in zip(refs[:count], refs[count:]):
        size = held.shape[1]
        out[...] = (held[...] + soon_ref[:, width : width + size].astype(F32)).astype(BF16)
        width += size


def final_kernel(direct, count, own_ref, soon_ref, *refs):
    straight, joined, out_ref = refs[:count], refs[count:-1], refs[-1]
    width = own_ref.shape[1]
    value = own_ref[...] + soon_ref[:, :width].astype(F32)
    for side, arrays in ((slice(0, direct), straight), (slice(direct, width), joined)):
        part = value[:, side]
        for came in arrays:
            part = part + came[...].astype(F32)
        out_ref[:, side] = part.astype(out_ref.dtype)


class Body:
    def __init__(self, groups, wide):
        self.groups, self.wide, self.chips = groups, wide, wide // 2
        self.last = None

    def call(self, kernel, ins, outs, scratch, flops, moved, limit, args):
        after = [] if self.last is None else [self.last]

        def run(*refs):
            kernel(*refs[len(after) :])

        got = pl.pallas_call(
            run,
            name=kernel.func.__name__ if isinstance(kernel, functools.partial) else kernel.__name__,
            in_specs=[STAY] * len(after) + ins,
            out_specs=[WHOLE] * len(outs),
            out_shape=outs,
            scratch_shapes=scratch,
            compiler_params=pltpu.CompilerParams(vmem_limit_bytes=limit),
            cost_estimate=pl.CostEstimate(flops=flops, bytes_accessed=moved, transcendentals=0),
        )(*after, *args)
        self.last = got[0]
        return got

    def other_core(self, value):
        return lax.ppermute(value, "wid", [(w, w ^ 1) for w in range(self.wide)])

    def along_x(self, value, j):
        return lax.ppermute(value, "wid", [(w, (w // 2 + j) % self.chips * 2 + w % 2) for w in range(self.wide)])

    def along_z(self, value, j):
        return lax.ppermute(value, "hid", [(z, z ^ j) for z in range(self.groups)])

    def gate_up_parts(self):
        parts = [p for h in self.parts for p in h]
        return parts, len(parts) * self.part

    def held_gate_up(self, pairs, ahead):
        weights = [w for pair in pairs for w in pair]
        parts, rows = self.gate_up_parts()
        size = sum(w.shape[1] for w in weights) // 2
        outs = [jax.ShapeDtypeStruct((2, 2, rows // 4, size), t) for t in (BF16, F32)]
        ins, more = [WHOLE] * (len(parts) + len(weights)), ()
        scratch = [pltpu.VMEM((rows, self.width), BF16)]
        if ahead is not None:
            outs += [jax.ShapeDtypeStruct((self.width, ahead[1]), BF16)] * 2
            ins, more = ins + [FAR] * 2, (self.gate_weight, self.up_weight)
            scratch.append(pltpu.SemaphoreType.DMA((2,)))
        got = self.call(
            functools.partial(held_gate_up_kernel, 2, self.groups // 2, len(pairs), None if ahead is None else ahead[0]),
            ins,
            outs,
            scratch,
            4 * rows * self.width * size,
            rows * self.width,
            6 * MIB,
            (*parts, *weights, *more),
        )
        return (got[1], self.other_core(got[0])), got[2:]

    def gate_up(self, start, size, weights, sends):
        parts, rows = self.gate_up_parts()
        width = self.width
        outs = [jax.ShapeDtypeStruct((2 // sends, 2, rows // 4, size), BF16)] * sends
        outs.append(jax.ShapeDtypeStruct((2, 2, rows // 4, size), F32))
        depth, slots = largest(width, (256, 128)), 16
        streamed = size - weights[0].shape[1]
        got = self.call(
            functools.partial(gate_up_kernel, start, size, depth, slots, 2, self.groups // 2, sends),
            [WHOLE] * (len(parts) + 2) + [FAR] * 2,
            outs,
            [
                pltpu.VMEM((rows, width), BF16),
                pltpu.VMEM((slots, depth, streamed), BF16),
                pltpu.SemaphoreType.DMA((slots,)),
            ],
            4 * rows * width * size,
            4 * width * size,
            26 * MIB,
            (*parts, *weights, self.gate_weight, self.up_weight),
        )
        return got[-1], *(self.other_core(v) for v in got[:-1])

    def fetch(self, start, size):
        return self.call(
            functools.partial(fetch_kernel, start),
            [FAR] * 2,
            [jax.ShapeDtypeStruct((self.width, size), BF16)] * 2,
            [pltpu.SemaphoreType.DMA((2,))],
            0,
            4 * self.width * size,
            2 * MIB,
            (self.gate_weight, self.up_weight),
        )

    def chip_sum(self, halves, args):
        size = args[0].shape[3]
        block = (len(halves), 2, self.block, size)
        own, *sends = self.call(
            functools.partial(chip_sum_kernel, self.chips, len(halves)),
            [WHOLE] * len(args),
            [jax.ShapeDtypeStruct(block, F32)] + [jax.ShapeDtypeStruct(block, BF16)] * (self.chips - 1),
            [],
            size * 256,
            size * 1024,
            4 * MIB,
            args,
        )
        return own, [self.along_x(v, j + 1) for j, v in enumerate(sends)]

    def hidden(self, summed):
        own, came = summed
        n, _, rows, size = own.shape
        (mine,) = self.call(
            hidden_kernel,
            [WHOLE] * (1 + len(came)),
            [jax.ShapeDtypeStruct((n, rows, size), BF16)],
            [],
            size * 256,
            size * 1024,
            4 * MIB,
            (own, *came),
        )
        return [mine] + [self.along_x(mine, j) for j in range(1, self.chips)]

    def pack(self, near):
        shape = jax.ShapeDtypeStruct((len(near),) + near[0].shape, BF16)
        (packed,) = self.call(pack_kernel, [WHOLE] * len(near), [shape], [], 256, 1024, 4 * MIB, near)
        return packed, self.other_core(packed)

    def fetch_rows(self, start, size):
        (rows,) = self.call(
            functools.partial(fetch_rows_kernel, start),
            [FAR],
            [jax.ShapeDtypeStruct((size, self.width), BF16)],
            [pltpu.SemaphoreType.DMA((1,))],
            0,
            2 * self.width * size,
            2 * MIB,
            (self.down_weight,),
        )
        return rows

    def down(self, packed, before, weights, direct=None):
        size = weights.shape[0]
        width, rows, part = self.width, 2 * self.half, self.part
        shape = jax.ShapeDtypeStruct
        if direct is None:
            outs = [shape((rows, width), F32)]
        else:
            pairs, joined = self.groups // 2 - 1, width - direct
            outs = [shape((part, width), F32), shape((part, width + pairs * joined), BF16)]
            outs += [shape((part, direct), BF16)] * (2 * pairs) + [shape((part, joined), F32)] * pairs
        return self.call(
            functools.partial(down_kernel, not before, direct),
            [WHOLE] * (3 + len(before)),
            outs,
            [pltpu.VMEM((rows, size), BF16)],
            2 * rows * width * size,
            rows * size,
            6 * MIB,
            (*packed, *before, weights),
        )

    def __call__(self, tokens, gate_weight, up_weight, down_weight):
        self.gate_weight, self.up_weight, self.down_weight = (
            pltpu.with_memory_space_constraint(w, pltpu.HBM) for w in (gate_weight, up_weight, down_weight)
        )
        self.part, self.width = tokens.shape
        groups = self.groups
        self.half = self.part * groups // 2
        self.block = self.half // self.wide
        units = gate_weight.shape[1]
        step = units // 26 if units // 26 % 128 == 0 else units // 13
        count = units // step
        cuts = [count * c // 26 * step for c in (0, 9, 17, 26)]
        (s0, n0), (s1, n1), (s2, n2) = [(a, b - a) for a, b in zip(cuts[:-1], cuts[1:])]
        both = (NEAR_ROWS, FAR_ROWS)

        blocks = [tokens] + [self.along_z(tokens, j) for j in range(1, groups)]
        self.parts = (blocks[: groups // 2], blocks[groups // 2 :])

        part = count * 6 // 26 * step
        w0 = self.fetch(s0, n0)
        w1 = self.fetch(s1, part)
        a0, rest = self.held_gate_up([w0], (s1 + part, n1 - part))
        a1, w2 = self.held_gate_up([w1, rest], (s2, count * 3 // 26 * step))
        b0 = self.chip_sum(both, a0)
        a2 = self.gate_up(s2, n2, w2, 2)
        b1 = self.chip_sum(both, a1)
        h0 = self.hidden(b0)
        b2 = self.chip_sum(both, a2)
        d0 = self.fetch_rows(s0, n0)
        h1 = self.hidden(b1)
        d1 = self.fetch_rows(s1, n1)
        p0 = self.pack(h0)
        d2 = self.fetch_rows(s2, n2)
        h2 = self.hidden(b2)
        value = self.down(p0, [], d0)
        p1 = self.pack(h1)
        p2 = self.pack(h2)
        value = self.down(p1, value, d1)
        direct = self.width // 128 * 10 // 16 * 128
        own, soon, *late = self.down(p2, value, d2, direct)
        straight, held = late[: groups - 2], late[groups - 2 :]
        soon = self.along_z(soon, 1)
        straight = [self.along_z(v, 2 + j) for j, v in enumerate(straight)]
        size = self.width - direct
        joined = self.call(
            functools.partial(pair_sum_kernel, self.width),
            [WHOLE] * (1 + len(held)),
            [jax.ShapeDtypeStruct((self.part, size), BF16)] * len(held),
            [],
            256,
            1024,
            4 * MIB,
            (soon, *held),
        )
        joined = [self.along_z(v, 2 + 2 * j) for j, v in enumerate(joined)]
        (mixed,) = self.call(
            functools.partial(final_kernel, direct, groups - 2),
            [WHOLE] * (2 + len(straight) + len(joined)),
            [jax.ShapeDtypeStruct((self.part, self.width), BF16)],
            [],
            256,
            1024,
            4 * MIB,
            (own, soon, *straight, *joined),
        )
        return mixed


def solution(mesh):
    placed = (P(("group", "hid"), "wid"), P("wid", "hid"), P("wid", "hid"), P("hid", "wid"))

    def run(*arrays):
        return Body(mesh.shape["hid"], mesh.shape["wid"])(*arrays)

    return jax.shard_map(run, mesh=mesh, in_specs=placed, out_specs=P(("group", "hid"), "wid"), check_vma=False)
```
